32 devices in a mesh: group: 2 (over y), batch: 4 (over z), bond: 4 (over x, core).
Axes of the slice: x: 2, y: 2, z: 4, core: 2. Of those that a mesh axis runs over, the one named last changes fastest.
Arguments:
- boundary: float32 [2048, 2048], P(('group', 'batch'), 'bond'), parts along dimension 0
- bits: int32 [2048, 3], P(('group', 'batch')), parts along dimension 0, may hold values from 0 to 1
- site_first: float32 [2, 2048, 2048], P(None, 'batch', 'bond'), may hold values from -0.125 to 0.125
- site_second: float32 [2, 2048, 2048], P(None, 'batch', 'bond'), may hold values from -0.125 to 0.125
- site_third: float32 [2, 2048, 2048], P(None, 'batch', 'bond'), may hold values from -0.125 to 0.125
Outputs:
- carried: float32 [2048, 2048], P(('group', 'batch'), 'bond'), parts along dimension 0
- log_scale: float32 [2048, 4], P(('group', 'batch')), parts along dimension 0
The draws below stay inside these ranges and needn't reach their ends.
There are 2 independent parts, one for each index of `group`. The reference program is written for one: setup_inputs(seed, part) draws one part's arguments, and reference() takes and returns one part's arrays. A program takes and returns all parts, laid end to end along the dimension named above; an argument that names none is the same for every part. Nothing has to cross between parts.
All inputs are finite; a program needn't handle non-finite values.
Results may differ from the reference program's by a relative error of at most 0.00013.
Values sent between devices are 32-bit elements; how exact they have to be, the bound alone decides.
No kernel may reach another device: no remote copies, remote signals or barrier semaphores. Data moves between devices by JAX's collectives and lax.ppermute only.
A program may use at most 128 MiB of HBM per device.

```python
import jax
import jax.numpy as jnp
from jax import lax

CHI = 2048
SITES = 3
ROWS = 1024


def draw_boundary(key, part):
    key = jax.random.fold_in(key, 1)
    key_rows, key_vals = jax.random.split(key, 2)
    rows = jnp.exp(jax.random.uniform(key_rows, (ROWS, 1), jnp.float32, -1.6, 1.6))
    values = jax.random.normal(key_vals, (ROWS, CHI), jnp.float32)
    values = jnp.clip(values, -6.0, 6.0)
    return (values * rows).astype(jnp.float32)


def touch_ends(array, stream_key, low, largest):
    longest = array.shape.index(max(array.shape))
    spots = []
    for shift in (0, 1):
        where = [jax.random.randint(jax.random.fold_in(stream_key, axis), (), 0, length) for axis, length in enumerate(array.shape)]
        where[longest] = (where[longest] + shift) % array.shape[longest]
        spots.append(tuple(where))
    return array.at[spots[0]].set(low).at[spots[1]].set(largest)


def shard_levels(key, dims, cuts, least, top_value):
    gain, own = 1.0, jax.random.fold_in(key, 6)
    for axis_at, shards_of in cuts:
        heights = jnp.exp(jax.random.uniform(jax.random.fold_in(own, axis_at), (shards_of,), jnp.float32, least / len(cuts), top_value / len(cuts)))
        gain = gain * jnp.repeat(heights, dims[axis_at] // shards_of).reshape([-1 if axis == axis_at else 1 for axis in range(len(dims))])
    return gain


def bell_draw(rng, extent, scale, most, cuts=(), dtype=jnp.bfloat16):
    gain = shard_levels(rng, extent, cuts, -0.22, 0.18) if cuts else 1.0
    result = jax.random.normal(rng, extent, jnp.float32) * scale * gain
    return jnp.minimum(jnp.maximum(result, -most), most).astype(dtype)


def setup_inputs(seed: int = 0, part: int = 0) -> dict:
    streams_of = jax.random.split(jax.random.key(seed), 6)
    own_keys = jax.random.split(jax.random.fold_in(streams_of[5], part), 6)
    boundary = draw_boundary(jax.random.fold_in(jax.random.fold_in(streams_of[5], part), 71), part)
    bits = touch_ends(jax.random.randint(own_keys[1], (ROWS, SITES), 0, 2), jax.random.fold_in(own_keys[1], 1), 0, 1).astype(jnp.int32)
    site_first = bell_draw(streams_of[2], (2, CHI, CHI), CHI ** -0.5, 0.125, ((1, 4), (2, 4)), jnp.float32)
    site_second = bell_draw(streams_of[3], (2, CHI, CHI), CHI ** -0.5, 0.125, ((1, 4), (2, 4)), jnp.float32)
    site_third = bell_draw(streams_of[4], (2, CHI, CHI), CHI ** -0.5, 0.125, ((1, 4), (2, 4)), jnp.float32)
    return {"boundary": boundary, "bits": bits, "site_first": site_first, "site_second": site_second, "site_third": site_third}


def row_scale(state):
    return jnp.sqrt(lax.optimization_barrier(jnp.sum(state * state, axis=1)) / CHI + 1e-06)

def reference(boundary, bits, site_first, site_second, site_third):
    state = boundary
    logs = []
    for index, site in enumerate((site_first, site_second, site_third)):
        scale = row_scale(state)
        logs.append(jnp.log(scale))
        state = state / scale[:, None]
        zero = jnp.dot(state, site[0], precision=lax.Precision.HIGHEST, preferred_element_type=jnp.float32)
        one = jnp.dot(state, site[1], precision=lax.Precision.HIGHEST, preferred_element_type=jnp.float32)
        state = jnp.where(bits[:, index][:, None] == 1, one, zero)
    scale = row_scale(state)
    logs.append(jnp.log(scale))
    return (state / scale[:, None], jnp.stack(logs, axis=1))
```

```python
import jax
import jax.numpy as jnp
from jax import lax
from jax.sharding import PartitionSpec as P


def site_product(state, tensor, bit):
    zero = jnp.dot(state, tensor[0], precision=lax.Precision.HIGH, preferred_element_type=jnp.float32)
    one = jnp.dot(state, tensor[1], precision=lax.Precision.HIGH, preferred_element_type=jnp.float32)
    return jnp.where((bit == 1)[:, None], one, zero)


def shards(boundary, bits, site_first, site_second, site_third):
    batch, bond = lax.axis_size("batch"), lax.axis_size("bond")
    here, side = lax.axis_index("batch"), lax.axis_index("bond")
    rows, columns = boundary.shape
    width = columns * bond
    part = rows // bond
    tensors = [lax.all_gather(t, "bond", axis=2, tiled=True) for t in (site_first, site_second, site_third)]
    own = lax.all_to_all(boundary, "bond", 0, 1, tiled=True)
    scale = jnp.sqrt(jnp.sum(own * own, axis=1) / width + 1e-06)
    first_log = jnp.log(scale)
    own = own / scale[:, None]
    state = lax.all_to_all(own, "batch", 1, 0, tiled=True)
    mine = lax.dynamic_slice_in_dim(bits, side * part, part, 0)
    picked = lax.all_gather(mine, "batch", axis=0, tiled=True)
    logs = []
    for index in range(2):
        state = site_product(state, tensors[index], picked[:, index])
        if index:
            state = state / scale[:, None]
        state = lax.psum_scatter(state, "batch", scatter_dimension=1, tiled=True)
        scale = jnp.sqrt(lax.psum(jnp.sum(state * state, axis=1), "batch") / width + 1e-06)
        logs.append(lax.dynamic_slice_in_dim(jnp.log(scale), here * part, part, 0))
    state = site_product(state, tensors[2], picked[:, 2]) / scale[:, None]
    state = lax.psum_scatter(state, "batch", scatter_dimension=0, tiled=True)
    scale = jnp.sqrt(jnp.sum(state * state, axis=1) / width + 1e-06)
    carried = lax.all_to_all(state / scale[:, None], "bond", 1, 0, tiled=True)
    logs = jnp.stack([first_log, *logs, jnp.log(scale)], axis=1)
    return carried, lax.all_gather(logs, "bond", axis=0, tiled=True)


def solution(mesh):
    return jax.shard_map(
        shards,
        mesh=mesh,
        in_specs=(
            P(("group", "batch"), "bond"),
            P(("group", "batch"), None),
            P(None, "batch", "bond"),
            P(None, "batch", "bond"),
            P(None, "batch", "bond"),
        ),
        out_specs=(P(("group", "batch"), "bond"), P(("group", "batch"), None)),
        check_vma=False,
    )
```

```python
import functools

import jax
import jax.numpy as jnp
from jax import lax
from jax.experimental import pallas as pl
from jax.experimental.pallas import tpu as pltpu
from jax.sharding import PartitionSpec as P

EXTRA = 8
STREAMS = 2


def pairs(size, distance):
    return [(i, i ^ distance) for i in range(size)]


def swap(value, axis, distance):
    return lax.ppermute(value, axis, pairs(lax.axis_size(axis), distance))


def pick(stack, index, axis=0):
    return lax.dynamic_index_in_dim(stack, index, axis, keepdims=False)


def reorder(stack, index):
    odd = (index & 1) == 1
    high = (index & 2) == 2
    a, b, c, d = stack
    a, b, c, d = (
        jnp.where(odd, b, a),
        jnp.where(odd, a, b),
        jnp.where(odd, d, c),
        jnp.where(odd, c, d),
    )
    return [jnp.where(high, c, a), jnp.where(high, d, b), jnp.where(high, a, c), jnp.where(high, b, d)]


def halves(value):
    high = value.astype(jnp.bfloat16)
    return high, (value - high.astype(jnp.float32)).astype(jnp.bfloat16)


def multiply(both, high, tensor):
    rows = high.shape[0]
    tensor_high, tensor_low = halves(tensor)
    wide = jnp.dot(both, tensor_high, preferred_element_type=jnp.float32)
    return wide[:rows] + wide[rows:] + jnp.dot(high, tensor_low, preferred_element_type=jnp.float32)


def product_kernel(site, last, where_ref, x_ref, bits_ref, own, core, far_a, far_b, cross_a, cross_b, out, held, sems):
    rows, left = x_ref.shape
    low, group = where_ref[0], where_ref[1]
    sources = ((own.at[0], own.at[1], far_a, far_b), (core.at[0], core.at[1], cross_a, cross_b))

    def copies(choice, first):
        return [
            pltpu.make_async_copy(ref, held.at[first + i], sems.at[first + i])
            for i, ref in enumerate(sources[choice])
        ]

    if last:
        for choice in (0, 1):
            for copy in copies(choice, 4 * choice):
                copy.start()
    else:
        for choice in (0, 1):

            @pl.when(low == choice)
            def _(choice=choice):
                for copy in copies(choice, 0):
                    copy.start()

    x = x_ref[...]
    high, rest = halves(x)
    both = jnp.concatenate([high, rest], axis=0)
    bit = bits_ref[:, site : site + 1]
    squares = jnp.sum(x * x, axis=1, keepdims=True)
    line = jnp.broadcast_to(squares, (rows, 128)).T[:EXTRA]
    below = jnp.concatenate([line, jnp.zeros((EXTRA, out.shape[2] - rows), jnp.float32)], axis=1)
    body = out.shape[1] - EXTRA
    for part in range(2):
        out[part, body:] = below
    for choice in range(2 if last else 1):
        waits = copies(choice, 4 * choice)
        for part in range(2):
            waits[2 * part].wait()
            first = multiply(both, high, held[4 * choice + 2 * part])
            waits[2 * part + 1].wait()
            second = multiply(both, high, held[4 * choice + 2 * part + 1])
            chosen = bit != (0 if part == 0 else group).astype(jnp.float32) if part else bit != 0.0
            value = jnp.where(chosen, second, first)
            if last:
                half = rows // 2
                block = 2 * part + choice
                for rows_set in range(2):
                    out[rows_set, block * half : (block + 1) * half] = value[rows_set * half : (rows_set + 1) * half]
            else:
                out[part, :body] = value


def product(site, last, place, x, bits, tiles):
    rows, left = x.shape
    right = tiles[0].shape[2]
    body = 2 * rows if last else rows
    count = 8 if last else 4
    vmem, anywhere = pl.BlockSpec(memory_space=pltpu.VMEM), pl.BlockSpec(memory_space=pl.ANY)
    return pl.pallas_call(
        functools.partial(product_kernel, site, last),
        out_shape=jax.ShapeDtypeStruct((2, body + EXTRA, right), jnp.float32),
        in_specs=[pl.BlockSpec(memory_space=pltpu.SMEM), vmem, vmem] + [anywhere] * 6,
        out_specs=vmem,
        scratch_shapes=[pltpu.VMEM((count, left, right), jnp.float32), pltpu.SemaphoreType.DMA((count,))],
        compiler_params=pltpu.CompilerParams(vmem_limit_bytes=32 * 1024 * 1024),
        cost_estimate=pl.CostEstimate(
            flops=2 * rows * left * right * count * 3, bytes_accessed=4 * left * right * count, transcendentals=0
        ),
    )(place, x, bits, *tiles)


def tile_gather(tensor, group):
    core = swap(tensor, "bond", 1)
    far_a = swap(pick(tensor, group), "bond", 2)
    far_b = swap(far_a, "group", 1)
    return [tensor, core, far_a, far_b, swap(far_a, "bond", 1), swap(far_b, "bond", 1)]


def shards_paired(boundary, bits, site_first, site_second, site_third):
    b, k, group = lax.axis_index("batch"), lax.axis_index("bond"), lax.axis_index("group")
    m = b ^ k
    rows, columns = boundary.shape
    width = columns * 4
    part = rows // 4
    piece = part // STREAMS

    blocks = boundary.reshape(4, part, columns)
    pieces = [pick(blocks, k)] + [swap(pick(blocks, k ^ d), "bond", d) for d in (1, 2, 3)]
    tiles = [tile_gather(t, group) for t in (site_first, site_second, site_third)]
    power = sum(jnp.sum(p * p, axis=1) for p in pieces)
    scale_first = jnp.sqrt(power / width + 1e-06)
    stack = jnp.stack(pieces) / scale_first[None, :, None]
    mine = lax.dynamic_slice_in_dim(bits, k * part, part, 0).astype(jnp.float32)
    line = jnp.pad(mine.T, ((0, EXTRA - 3), (0, columns - part)))
    sent = [jnp.concatenate([pick(stack, m ^ d), line], axis=0) for d in range(4)]
    got = reorder([sent[0]] + [swap(sent[d], "batch", d) for d in (1, 2, 3)], b)
    state = [jnp.concatenate([g[t * piece : (t + 1) * piece] for g in got], axis=0) for t in range(STREAMS)]
    marks = [
        jnp.concatenate([g[part : part + 3, t * piece : (t + 1) * piece] for g in got], axis=1).T
        for t in range(STREAMS)
    ]

    low, high = m & 1, (m >> 1) & 1
    logs = [[jnp.log(scale_first[t * piece : (t + 1) * piece])] for t in range(STREAMS)]
    results = []
    for site in range(3):
        for t in range(STREAMS):
            x, mark = state[t], marks[t]
            count = x.shape[0]
            if site < 2:
                sent = product(site, False, jnp.stack([1 - low, group]), x, mark, tiles[site])
                kept = product(site, False, jnp.stack([low, group]), x, mark, tiles[site])
                upper = high
            else:
                sets = x.reshape(2, 2, piece, columns)
                mark_sets = mark.reshape(2, 2, piece, 3)
                sent, kept = [
                    product(
                        site,
                        True,
                        jnp.stack([low, group]),
                        pick(sets, i, 1).reshape(2 * piece, columns),
                        pick(mark_sets, i, 1).reshape(2 * piece, 3),
                        tiles[site],
                    )
                    for i in (1 - (b & 1), b & 1)
                ]
                upper = (b >> 1) & 1
            got = swap(sent, "batch", 1)
            away = pick(kept, 1 - upper) + pick(got, 1 - upper)
            total = pick(kept, upper) + pick(got, upper) + swap(away, "batch", 2)
            if site == 0:
                state[t] = total[:-EXTRA]
                continue
            if site == 1:
                scale = jnp.sqrt(total[-EXTRA, :count] / width + 1e-06)
                state[t] = total[:-EXTRA] / scale[:, None]
                logs[t].append(jnp.log(lax.dynamic_slice_in_dim(scale, b * piece, piece, 0)))
                continue
            scale = jnp.sqrt(lax.dynamic_slice_in_dim(total[-EXTRA], upper * piece, piece, 0) / width + 1e-06)
            logs[t].append(jnp.log(scale))
            value = total[:-EXTRA].reshape(4, piece, columns) / scale[None, :, None]
            scale = jnp.sqrt(jnp.sum(value * value, axis=(0, 2)) / width + 1e-06)
            logs[t].append(jnp.log(scale))
            value = value / scale[None, :, None]
            line = jnp.pad(jnp.stack(logs[t]), ((0, EXTRA - 4), (0, columns - piece)))
            out = [jnp.concatenate([value[d], line], axis=0) for d in range(4)]
            results.append(reorder([out[0]] + [swap(out[d], "bond", d) for d in (1, 2, 3)], k))
    carried = jnp.concatenate([results[t][i][:piece] for i in range(4) for t in range(STREAMS)], axis=0)
    log_scale = jnp.concatenate([results[t][i][piece : piece + 4, :piece] for i in range(4) for t in range(STREAMS)], axis=1)
    return carried, log_scale.T


def site_product(state, tensor, bit):
    zero = jnp.dot(state, tensor[0], precision=lax.Precision.HIGH, preferred_element_type=jnp.float32)
    one = jnp.dot(state, tensor[1], precision=lax.Precision.HIGH, preferred_element_type=jnp.float32)
    return jnp.where((bit == 1)[:, None], one, zero)


def shards_any(boundary, bits, site_first, site_second, site_third):
    bond = lax.axis_size("bond")
    here, side = lax.axis_index("batch"), lax.axis_index("bond")
    rows, columns = boundary.shape
    width = columns * bond
    part = rows // bond
    tensors = [lax.all_gather(t, "bond", axis=2, tiled=True) for t in (site_first, site_second, site_third)]
    own = lax.all_to_all(boundary, "bond", 0, 1, tiled=True)
    scale = jnp.sqrt(jnp.sum(own * own, axis=1) / width + 1e-06)
    first_log = jnp.log(scale)
    own = own / scale[:, None]
    state = lax.all_to_all(own, "batch", 1, 0, tiled=True)
    mine = lax.dynamic_slice_in_dim(bits, side * part, part, 0)
    picked = lax.all_gather(mine, "batch", axis=0, tiled=True)
    logs = []
    for index in range(2):
        state = site_product(state, tensors[index], picked[:, index])
        if index:
            state = state / scale[:, None]
        state = lax.psum_scatter(state, "batch", scatter_dimension=1, tiled=True)
        scale = jnp.sqrt(lax.psum(jnp.sum(state * state, axis=1), "batch") / width + 1e-06)
        logs.append(lax.dynamic_slice_in_dim(jnp.log(scale), here * part, part, 0))
    state = site_product(state, tensors[2], picked[:, 2]) / scale[:, None]
    state = lax.psum_scatter(state, "batch", scatter_dimension=0, tiled=True)
    scale = jnp.sqrt(jnp.sum(state * state, axis=1) / width + 1e-06)
    carried = lax.all_to_all(state / scale[:, None], "bond", 1, 0, tiled=True)
    logs = jnp.stack([first_log, *logs, jnp.log(scale)], axis=1)
    return carried, lax.all_gather(logs, "bond", axis=0, tiled=True)


def solution(mesh):
    sizes = (mesh.shape["group"], mesh.shape["batch"], mesh.shape["bond"])
    return jax.shard_map(
        shards_paired if sizes == (2, 4, 4) else shards_any,
        mesh=mesh,
        in_specs=(
            P(("group", "batch"), "bond"),
            P(("group", "batch"), None),
            P(None, "batch", "bond"),
            P(None, "batch", "bond"),
            P(None, "batch", "bond"),
        ),
        out_specs=(P(("group", "batch"), "bond"), P(("group", "batch"), None)),
        check_vma=False,
    )
```

```python
import functools

import jax
import jax.numpy as jnp
from jax import lax
from jax.experimental import pallas as pl
from jax.experimental.pallas import tpu as pltpu
from jax.sharding import PartitionSpec as P

EXTRA = 8
VMEM = 48 * 1024 * 1024
COST = 1
RESIDENT = (False, False, False)


def pairs(size, distance):
    return [(i, i ^ distance) for i in range(size)]


def swap(value, axis, distance):
    return lax.ppermute(value, axis, pairs(lax.axis_size(axis), distance))


def pick(stack, index, axis=0):
    return lax.dynamic_index_in_dim(stack, index, axis, keepdims=False)


def reorder(stack, index):
    odd = (index & 1) == 1
    high = (index & 2) == 2
    a, b, c, d = stack
    a, b, c, d = (
        jnp.where(odd, b, a),
        jnp.where(odd, a, b),
        jnp.where(odd, d, c),
        jnp.where(odd, c, d),
    )
    return [jnp.where(high, c, a), jnp.where(high, d, b), jnp.where(high, a, c), jnp.where(high, b, d)]


def tie(*values):
    return lax.optimization_barrier(values)


def halves(value):
    high = value.astype(jnp.bfloat16)
    return high, (value - high.astype(jnp.float32)).astype(jnp.bfloat16)


def product_kernel(site, every, extra, cut, resident, place_ref, x_ref, bits_ref, *refs):
    near, far, out, tensor_high, tensor_low, *rest = refs[:2], refs[2:8], *refs[8:]
    rows, left = x_ref.shape
    block, group = place_ref[0], place_ref[1]
    spans = ((0, cut), (cut, left - cut))

    def sources(option):
        if option < 2:
            return [[near[option].at[i, pl.ds(at, size)] for at, size in spans] for i in (0, 1)]
        first, second, others = far[option - 2 :: 2]
        return [[first, others.at[group]], [second, others.at[1 - group]]]

    def copies(option, slot, i):
        held, sems = rest
        return [
            pltpu.make_async_copy(source, held.at[slot + i, pl.ds(at, size)], sems.at[slot + i, j])
            for j, (source, (at, size)) in enumerate(zip(sources(option)[i], spans))
        ]

    def start(option, slot):
        for i in (0, 1):
            for copy in copies(option, slot, i):
                copy.start()

    if not resident:
        for option in range(4):
            if every:
                start(option, 2 * option)
            else:
                pl.when(block == option)(functools.partial(start, option, 0))

    def split(option, i):
        for source, (at, size) in zip(sources(option)[i], spans):
            tensor_high[i, at : at + size], tensor_low[i, at : at + size] = halves(source[...])

    x = x_ref[...]
    high, lower = halves(x)
    both = jnp.concatenate([high, lower], axis=0)
    bit = bits_ref[:, site : site + 1]
    if extra:
        squares = jnp.sum(x * x, axis=1, keepdims=True)
        line = jnp.broadcast_to(squares, (rows, 128)).T[:EXTRA]
        out[out.shape[0] - EXTRA :] = jnp.concatenate(
            [line, jnp.zeros((EXTRA, out.shape[1] - rows), jnp.float32)], axis=1
        )
    for option in range(4) if every else (None,):
        slot = 2 * (option or 0)
        values = []
        for i in (0, 1):
            if not resident:
                for copy in copies(option or 0, slot, i):
                    copy.wait()
                tensor_high[i], tensor_low[i] = halves(rest[0][slot + i])
            elif every:
                split(option, i)
            else:
                for choice in range(4):
                    pl.when(block == choice)(functools.partial(split, choice, i))
            wide = jnp.dot(both, tensor_high[i], preferred_element_type=jnp.float32)
            narrow = jnp.dot(high, tensor_low[i], preferred_element_type=jnp.float32)
            values.append(wide[:rows] + wide[rows:] + narrow)
        is_far = (option >= 2) if every else (block >= 2)
        own_bit = group.astype(jnp.float32)
        first_bit = jnp.where(is_far, own_bit, 0.0)
        value = jnp.where(bit != first_bit, values[1], values[0])
        at = (option or 0) * rows
        out[at : at + rows] = value


def product(site, every, extra, block, group, x, bits, tiles):
    rows, left = x.shape
    right = x.shape[1]
    blocks = 4 if every else 1
    resident = RESIDENT[site]
    vmem = pl.BlockSpec(memory_space=pltpu.VMEM)
    given = vmem if resident else pl.BlockSpec(memory_space=pl.ANY)
    scratch = [pltpu.VMEM((2, left, right), jnp.bfloat16)] * 2
    if not resident:
        scratch += [pltpu.VMEM((2 * blocks, left, right), jnp.float32), pltpu.SemaphoreType.DMA((2 * blocks, 2))]
    return pl.pallas_call(
        functools.partial(product_kernel, site, every, extra, tiles[2].shape[0], resident),
        out_shape=jax.ShapeDtypeStruct((blocks * rows + (EXTRA if extra else 0), right), jnp.float32),
        in_specs=[pl.BlockSpec(memory_space=pltpu.SMEM), vmem, vmem] + [given] * len(tiles),
        out_specs=vmem,
        scratch_shapes=scratch,
        compiler_params=pltpu.CompilerParams(vmem_limit_bytes=VMEM),
        cost_estimate=pl.CostEstimate(flops=COST, bytes_accessed=COST, transcendentals=0),
    )(jnp.stack([block, group]), x, bits, *tiles)


def start_x(tensor, group):
    return swap(pick(tensor, group)[: tensor.shape[1] * 11 // 16], "bond", 2)


def start_rest(tensor):
    return swap(tensor[:, tensor.shape[1] * 11 // 16 :], "bond", 2)


def shards_paired(boundary, bits, site_first, site_second, site_third):
    b, k, group = lax.axis_index("batch"), lax.axis_index("bond"), lax.axis_index("group")
    m = b ^ k
    rows, columns = boundary.shape
    width = columns * 4
    part = rows // 4

    blocks = boundary.reshape(4, part, columns)
    p2, p3, p1 = [swap(pick(blocks, k ^ d), "bond", d) for d in (2, 3, 1)]
    p1, p2, p3, t1 = tie(p1, p2, p3, site_first)
    x1 = start_x(t1, group)
    pieces = [pick(blocks, k), p1, p2, p3]
    power = sum(jnp.sum(p * p, axis=1) for p in pieces)
    scale_first = jnp.sqrt(power / width + 1e-06)
    stack = jnp.stack(pieces) / scale_first[None, :, None]
    mine = lax.dynamic_slice_in_dim(bits, k * part, part, 0).astype(jnp.float32)
    line = jnp.pad(mine.T, ((0, EXTRA - 3), (0, columns - part)))
    sent = [jnp.concatenate([pick(stack, m ^ d), line], axis=0) for d in range(4)]
    arrived = [sent[0]] + [swap(sent[d], "batch", d) for d in (1, 2, 3)]
    got = reorder(arrived, b)
    state = jnp.concatenate([g[:part] for g in got], axis=0)
    marks = jnp.concatenate([g[part : part + 3, :part] for g in got], axis=1).T
    logs = [jnp.log(scale_first)]

    x1, t1, state = tie(x1, t1, state)
    y1, rest1, cross_x1 = swap(x1, "group", 1), start_rest(t1), swap(x1, "bond", 1)
    core1 = swap(t1, "bond", 1)
    y1, rest1, cross_x1, t2 = tie(y1, rest1, cross_x1, site_second)
    tiles = [t1, core1, x1, cross_x1, y1, swap(y1, "bond", 1), rest1, swap(rest1, "bond", 1)]
    x2, core2 = start_x(t2, group), swap(t2, "bond", 1)

    def batch_sum(site, x, extra, tiles, *more):
        def one(r):
            return product(site, False, extra, r, group, x, marks, tiles)

        fwd_got = swap(one(m ^ 3), "batch", 1)
        fwd_kept, stay_sent = one(m ^ 2), one(m ^ 1)
        fwd_got, fwd_kept, stay_sent, *more = tie(fwd_got, fwd_kept, stay_sent, *more)
        came = swap(fwd_kept + fwd_got, "batch", 2)
        stay_got = swap(stay_sent, "batch", 1)
        return lambda: one(m) + stay_got + came, more

    def settle(total):
        scale = jnp.sqrt(total[-EXTRA, :rows] / width + 1e-06)
        logs.append(jnp.log(lax.dynamic_slice_in_dim(scale, b * part, part, 0)))
        return total[:-EXTRA] / scale[:, None]

    total, (x2, t2, core2) = batch_sum(0, state, False, tiles, x2, t2, core2)
    y2, rest2, cross_x2 = swap(x2, "group", 1), start_rest(t2), swap(x2, "bond", 1)
    y2, rest2, cross_x2, t3 = tie(y2, rest2, cross_x2, site_third)
    tiles = [t2, core2, x2, cross_x2, y2, swap(y2, "bond", 1), rest2, swap(rest2, "bond", 1)]
    x3 = start_x(t3, group)
    state, t3 = tie(total(), t3)
    core3 = swap(t3, "bond", 1)

    total, (x3, t3, core3) = batch_sum(1, state, True, tiles, x3, t3, core3)
    y3, rest3, cross_x3 = swap(x3, "group", 1), start_rest(t3), swap(x3, "bond", 1)
    y3, rest3, cross_x3 = tie(y3, rest3, cross_x3)
    tiles = [t3, core3, x3, cross_x3, y3, swap(y3, "bond", 1), rest3, swap(rest3, "bond", 1)]
    state = settle(total())

    def last(d):
        x = pick(state.reshape(4, part, columns), b ^ d)
        mark = pick(marks.reshape(4, part, 3), b ^ d)
        return product(2, True, True, b, group, x, mark, tiles)

    fwd_got = swap(last(3), "batch", 1)
    fwd_kept, stay_sent = last(2), last(1)
    fwd_got, fwd_kept, stay_sent = tie(fwd_got, fwd_kept, stay_sent)
    came = swap(fwd_kept + fwd_got, "batch", 2)
    stay_got = swap(stay_sent, "batch", 1)
    total = last(0) + stay_got + came
    scale = jnp.sqrt(total[-EXTRA, :part] / width + 1e-06)
    logs.append(jnp.log(scale))
    value = total[:-EXTRA].reshape(4, part, columns) / scale[None, :, None]
    scale = jnp.sqrt(jnp.sum(value * value, axis=(0, 2)) / width + 1e-06)
    logs.append(jnp.log(scale))
    value = value / scale[None, :, None]
    line = jnp.pad(jnp.stack(logs), ((0, EXTRA - 4), (0, columns - part)))
    out = [jnp.concatenate([value[d], line], axis=0) for d in range(4)]
    result = reorder([out[0]] + [swap(out[d], "bond", d) for d in (1, 2, 3)], k)
    carried = jnp.concatenate([r[:part] for r in result], axis=0)
    return carried, jnp.concatenate([r[part : part + 4, :part] for r in result], axis=1).T


def site_product(state, tensor, bit):
    zero = jnp.dot(state, tensor[0], precision=lax.Precision.HIGH, preferred_element_type=jnp.float32)
    one = jnp.dot(state, tensor[1], precision=lax.Precision.HIGH, preferred_element_type=jnp.float32)
    return jnp.where((bit == 1)[:, None], one, zero)


def shards_any(boundary, bits, site_first, site_second, site_third):
    bond = lax.axis_size("bond")
    here, side = lax.axis_index("batch"), lax.axis_index("bond")
    rows, columns = boundary.shape
    width = columns * bond
    part = rows // bond
    tensors = [lax.all_gather(t, "bond", axis=2, tiled=True) for t in (site_first, site_second, site_third)]
    own = lax.all_to_all(boundary, "bond", 0, 1, tiled=True)
    scale = jnp.sqrt(jnp.sum(own * own, axis=1) / width + 1e-06)
    first_log = jnp.log(scale)
    own = own / scale[:, None]
    state = lax.all_to_all(own, "batch", 1, 0, tiled=True)
    mine = lax.dynamic_slice_in_dim(bits, side * part, part, 0)
    picked = lax.all_gather(mine, "batch", axis=0, tiled=True)
    logs = []
    for index in range(2):
        state = site_product(state, tensors[index], picked[:, index])
        if index:
            state = state / scale[:, None]
        state = lax.psum_scatter(state, "batch", scatter_dimension=1, tiled=True)
        scale = jnp.sqrt(lax.psum(jnp.sum(state * state, axis=1), "batch") / width + 1e-06)
        logs.append(lax.dynamic_slice_in_dim(jnp.log(scale), here * part, part, 0))
    state = site_product(state, tensors[2], picked[:, 2]) / scale[:, None]
    state = lax.psum_scatter(state, "batch", scatter_dimension=0, tiled=True)
    scale = jnp.sqrt(jnp.sum(state * state, axis=1) / width + 1e-06)
    carried = lax.all_to_all(state / scale[:, None], "bond", 1, 0, tiled=True)
    logs = jnp.stack([first_log, *logs, jnp.log(scale)], axis=1)
    return carried, lax.all_gather(logs, "bond", axis=0, tiled=True)


def solution(mesh):
    sizes = (mesh.shape["group"], mesh.shape["batch"], mesh.shape["bond"])
    return jax.shard_map(
        shards_paired if sizes == (2, 4, 4) else shards_any,
        mesh=mesh,
        in_specs=(
            P(("group", "batch"), "bond"),
            P(("group", "batch"), None),
            P(None, "batch", "bond"),
            P(None, "batch", "bond"),
            P(None, "batch", "bond"),
        ),
        out_specs=(P(("group", "batch"), "bond"), P(("group", "batch"), None)),
        check_vma=False,
    )
```

```python
import functools

import jax
import jax.numpy as jnp
from jax import lax
from jax.experimental import pallas as pl
from jax.experimental.pallas import tpu as pltpu
from jax.sharding import PartitionSpec as P

EXTRA = 8
VMEM = 48 * 1024 * 1024
COST = 1
RESIDENT = (False, False, False)


def pairs(size, distance):
    return [(i, i ^ distance) for i in range(size)]


def swap(value, axis, distance):
    return lax.ppermute(value, axis, pairs(lax.axis_size(axis), distance))


def pick(stack, index, axis=0):
    return lax.dynamic_index_in_dim(stack, index, axis, keepdims=False)


def reorder(stack, index):
    odd = (index & 1) == 1
    high = (index & 2) == 2
    a, b, c, d = stack
    a, b, c, d = (
        jnp.where(odd, b, a),
        jnp.where(odd, a, b),
        jnp.where(odd, d, c),
        jnp.where(odd, c, d),
    )
    return [jnp.where(high, c, a), jnp.where(high, d, b), jnp.where(high, a, c), jnp.where(high, b, d)]


def tie(*values):
    return lax.optimization_barrier(values)


def halves(value):
    high = value.astype(jnp.bfloat16)
    return high, (value - high.astype(jnp.float32)).astype(jnp.bfloat16)


def product_kernel(site, every, extra, cut, resident, place_ref, x_ref, bits_ref, *refs):
    near, far, out, tensor_high, tensor_low, *rest = refs[:2], refs[2:8], *refs[8:]
    rows, left = x_ref.shape
    block, group = place_ref[0], place_ref[1]
    spans = ((0, cut), (cut, left - cut))

    def sources(option):
        if option < 2:
            return [[near[option].at[i, pl.ds(at, size)] for at, size in spans] for i in (0, 1)]
        first, second, others = far[option - 2 :: 2]
        return [[first, others.at[group]], [second, others.at[1 - group]]]

    def copies(option, slot, i):
        held, sems = rest
        return [
            pltpu.make_async_copy(source, held.at[slot + i, pl.ds(at, size)], sems.at[slot + i, j])
            for j, (source, (at, size)) in enumerate(zip(sources(option)[i], spans))
        ]

    def start(option, slot):
        for i in (0, 1):
            for copy in copies(option, slot, i):
                copy.start()

    if not resident:
        for option in range(4):
            if every:
                start(option, 2 * option)
            else:
                pl.when(block == option)(functools.partial(start, option, 0))

    def split(option, i):
        for source, (at, size) in zip(sources(option)[i], spans):
            tensor_high[i, at : at + size], tensor_low[i, at : at + size] = halves(source[...])

    x = x_ref[...]
    high, lower = halves(x)
    both = jnp.concatenate([high, lower], axis=0)
    bit = bits_ref[:, site : site + 1]
    if extra:
        squares = jnp.sum(x * x, axis=1, keepdims=True)
        line = jnp.broadcast_to(squares, (rows, 128)).T[:EXTRA]
        out[out.shape[0] - EXTRA :] = jnp.concatenate(
            [line, jnp.zeros((EXTRA, out.shape[1] - rows), jnp.float32)], axis=1
        )
    for option in range(4) if every else (None,):
        slot = 2 * (option or 0)
        values = []
        for i in (0, 1):
            if not resident:
                for copy in copies(option or 0, slot, i):
                    copy.wait()
                tensor_high[i], tensor_low[i] = halves(rest[0][slot + i])
            elif every:
                split(option, i)
            else:
                for choice in range(4):
                    pl.when(block == choice)(functools.partial(split, choice, i))
            wide = jnp.dot(both, tensor_high[i], preferred_element_type=jnp.float32)
            narrow = jnp.dot(high, tensor_low[i], preferred_element_type=jnp.float32)
            values.append(wide[:rows] + wide[rows:] + narrow)
        is_far = (option >= 2) if every else (block >= 2)
        own_bit = group.astype(jnp.float32)
        first_bit = jnp.where(is_far, own_bit, 0.0)
        value = jnp.where(bit != first_bit, values[1], values[0])
        at = (option or 0) * rows
        out[at : at + rows] = value


def product(site, every, extra, block, group, x, bits, tiles):
    rows, left = x.shape
    right = x.shape[1]
    blocks = 4 if every else 1
    resident = RESIDENT[site]
    vmem = pl.BlockSpec(memory_space=pltpu.VMEM)
    given = vmem if resident else pl.BlockSpec(memory_space=pl.ANY)
    scratch = [pltpu.VMEM((2, left, right), jnp.bfloat16)] * 2
    if not resident:
        scratch += [pltpu.VMEM((2 * blocks, left, right), jnp.float32), pltpu.SemaphoreType.DMA((2 * blocks, 2))]
    return pl.pallas_call(
        functools.partial(product_kernel, site, every, extra, tiles[2].shape[0], resident),
        out_shape=jax.ShapeDtypeStruct((blocks * rows + (EXTRA if extra else 0), right), jnp.float32),
        in_specs=[pl.BlockSpec(memory_space=pltpu.SMEM), vmem, vmem] + [given] * len(tiles),
        out_specs=vmem,
        scratch_shapes=scratch,
        compiler_params=pltpu.CompilerParams(vmem_limit_bytes=VMEM),
        cost_estimate=pl.CostEstimate(flops=COST, bytes_accessed=COST, transcendentals=0),
    )(jnp.stack([block, group]), x, bits, *tiles)


def parts_over_x(tensor, group):
    cut = tensor.shape[1] * 11 // 16
    return pick(tensor, group)[:cut], tensor[:, cut:]


def shards_paired(boundary, bits, site_first, site_second, site_third):
    b, k, group = lax.axis_index("batch"), lax.axis_index("bond"), lax.axis_index("group")
    m = b ^ k
    rows, columns = boundary.shape
    width = columns * 4
    part = rows // 4

    blocks = boundary.reshape(4, part, columns)
    p2, p3, p1 = [swap(pick(blocks, k ^ d), "bond", d) for d in (2, 3, 1)]
    most, remains = parts_over_x(site_first, group)
    x1, core1 = swap(most, "bond", 2), swap(site_first, "bond", 1)
    pieces = [pick(blocks, k), p1, p2, p3]
    power = sum(jnp.sum(p * p, axis=1) for p in pieces)
    scale_first = jnp.sqrt(power / width + 1e-06)
    stack = jnp.stack(pieces) / scale_first[None, :, None]
    mine = lax.dynamic_slice_in_dim(bits, k * part, part, 0).astype(jnp.float32)
    line = jnp.pad(mine.T, ((0, EXTRA - 3), (0, columns - part)))
    sent = [jnp.concatenate([pick(stack, m ^ d), line], axis=0) for d in range(4)]
    arrived = [sent[0]] + [swap(sent[d], "batch", d) for d in (1, 2, 3)]
    got = reorder(arrived, b)
    state = jnp.concatenate([g[:part] for g in got], axis=0)
    marks = jnp.concatenate([g[part : part + 3, :part] for g in got], axis=1).T
    logs = [jnp.log(scale_first)]

    x1, remains, core1 = tie(x1, remains, core1)
    t1, y1, rest1 = site_first, swap(x1, "group", 1), swap(remains, "bond", 2)
    most, remains = parts_over_x(site_second, group)
    y1, rest1, state, x1, most = tie(y1, rest1, state, x1, most)
    t2 = site_second
    tiles = [t1, core1, x1, swap(x1, "bond", 1), y1, swap(y1, "bond", 1), rest1, swap(rest1, "bond", 1)]
    x2, core2 = swap(most, "bond", 2), swap(t2, "bond", 1)

    def batch_sum(site, x, extra, tiles, *more):
        def one(r):
            return product(site, False, extra, r, group, x, marks, tiles)

        fwd_got = swap(one(m ^ 3), "batch", 1)
        fwd_kept, stay_sent = one(m ^ 2), one(m ^ 1)
        away, stay_sent, *more = tie(fwd_kept + fwd_got, stay_sent, *more)
        came = swap(away, "batch", 2)
        stay_got = swap(stay_sent, "batch", 1)
        return one(m), stay_got, came, more

    def settle(total):
        scale = jnp.sqrt(total[-EXTRA, :rows] / width + 1e-06)
        logs.append(jnp.log(lax.dynamic_slice_in_dim(scale, b * part, part, 0)))
        return total[:-EXTRA] / scale[:, None]

    kept, stayed, came, (x2, t2, core2, remains) = batch_sum(0, state, False, tiles, x2, t2, core2, remains)
    y2, rest2, cross_x2 = swap(x2, "group", 1), swap(remains, "bond", 2), swap(x2, "bond", 1)
    most, remains = parts_over_x(site_third, group)
    y2, rest2, cross_x2, most, stayed, came = tie(y2, rest2, cross_x2, most, stayed, came)
    t3 = site_third
    tiles = [t2, core2, x2, cross_x2, y2, swap(y2, "bond", 1), rest2, swap(rest2, "bond", 1)]
    x3 = swap(most, "bond", 2)
    state, t3 = tie(kept + stayed + came, t3)
    core3 = swap(t3, "bond", 1)

    kept, stayed, came, (x3, t3, core3, remains) = batch_sum(1, state, True, tiles, x3, t3, core3, remains)
    y3, rest3, cross_x3 = swap(x3, "group", 1), swap(remains, "bond", 2), swap(x3, "bond", 1)
    y3, rest3, cross_x3 = tie(y3, rest3, cross_x3)
    tiles = [t3, core3, x3, cross_x3, y3, swap(y3, "bond", 1), rest3, swap(rest3, "bond", 1)]
    state = settle(kept + stayed + came)

    def last(d):
        x = pick(state.reshape(4, part, columns), b ^ d)
        mark = pick(marks.reshape(4, part, 3), b ^ d)
        return product(2, True, True, b, group, x, mark, tiles)

    fwd_got = swap(last(3), "batch", 1)
    fwd_kept, stay_sent = last(2), last(1)
    fwd_got, fwd_kept, stay_sent = tie(fwd_got, fwd_kept, stay_sent)
    came = swap(fwd_kept + fwd_got, "batch", 2)
    stay_got = swap(stay_sent, "batch", 1)
    total = last(0) + stay_got + came
    scale = jnp.sqrt(total[-EXTRA, :part] / width + 1e-06)
    logs.append(jnp.log(scale))
    value = total[:-EXTRA].reshape(4, part, columns) / scale[None, :, None]
    scale = jnp.sqrt(jnp.sum(value * value, axis=(0, 2)) / width + 1e-06)
    logs.append(jnp.log(scale))
    value = value / scale[None, :, None]
    line = jnp.pad(jnp.stack(logs), ((0, EXTRA - 4), (0, columns - part)))
    out = [jnp.concatenate([value[d], line], axis=0) for d in range(4)]
    result = reorder([out[0]] + [swap(out[d], "bond", d) for d in (1, 2, 3)], k)
    carried = jnp.concatenate([r[:part] for r in result], axis=0)
    return carried, jnp.concatenate([r[part : part + 4, :part] for r in result], axis=1).T


def site_product(state, tensor, bit):
    zero = jnp.dot(state, tensor[0], precision=lax.Precision.HIGH, preferred_element_type=jnp.float32)
    one = jnp.dot(state, tensor[1], precision=lax.Precision.HIGH, preferred_element_type=jnp.float32)
    return jnp.where((bit == 1)[:, None], one, zero)


def shards_any(boundary, bits, site_first, site_second, site_third):
    bond = lax.axis_size("bond")
    here, side = lax.axis_index("batch"), lax.axis_index("bond")
    rows, columns = boundary.shape
    width = columns * bond
    part = rows // bond
    tensors = [lax.all_gather(t, "bond", axis=2, tiled=True) for t in (site_first, site_second, site_third)]
    own = lax.all_to_all(boundary, "bond", 0, 1, tiled=True)
    scale = jnp.sqrt(jnp.sum(own * own, axis=1) / width + 1e-06)
    first_log = jnp.log(scale)
    own = own / scale[:, None]
    state = lax.all_to_all(own, "batch", 1, 0, tiled=True)
    mine = lax.dynamic_slice_in_dim(bits, side * part, part, 0)
    picked = lax.all_gather(mine, "batch", axis=0, tiled=True)
    logs = []
    for index in range(2):
        state = site_product(state, tensors[index], picked[:, index])
        if index:
            state = state / scale[:, None]
        state = lax.psum_scatter(state, "batch", scatter_dimension=1, tiled=True)
        scale = jnp.sqrt(lax.psum(jnp.sum(state * state, axis=1), "batch") / width + 1e-06)
        logs.append(lax.dynamic_slice_in_dim(jnp.log(scale), here * part, part, 0))
    state = site_product(state, tensors[2], picked[:, 2]) / scale[:, None]
    state = lax.psum_scatter(state, "batch", scatter_dimension=0, tiled=True)
    scale = jnp.sqrt(jnp.sum(state * state, axis=1) / width + 1e-06)
    carried = lax.all_to_all(state / scale[:, None], "bond", 1, 0, tiled=True)
    logs = jnp.stack([first_log, *logs, jnp.log(scale)], axis=1)
    return carried, lax.all_gather(logs, "bond", axis=0, tiled=True)


def solution(mesh):
    sizes = (mesh.shape["group"], mesh.shape["batch"], mesh.shape["bond"])
    return jax.shard_map(
        shards_paired if sizes == (2, 4, 4) else shards_any,
        mesh=mesh,
        in_specs=(
            P(("group", "batch"), "bond"),
            P(("group", "batch"), None),
            P(None, "batch", "bond"),
            P(None, "batch", "bond"),
            P(None, "batch", "bond"),
        ),
        out_specs=(P(("group", "batch"), "bond"), P(("group", "batch"), None)),
        check_vma=False,
    )
```
